256 devices in a mesh: grp: 16 (over x, y_lo, core), wk: 16 (over z, y_hi).
Axes of the slice: x: 4, y: 4 (y_hi: 2, y_lo: 2; y = y_hi * 2 + y_lo), z: 8, core: 2. Of those that a mesh axis runs over, the one named last changes fastest.
Arguments:
- owned_layer: int32 [16], replicated, may hold values from 0 to 15, each once
- wide_side: bfloat16 [16, 32768, 1024], P(None, ('grp', 'wk')), may hold values from -24 to 24
- narrow_side: bfloat16 [16, 32768, 256], P(None, ('grp', 'wk')), may hold values from -6 to 6
- wide_basis: float32 [16, 1024, 1024], P('grp', 'wk'), may hold values from -0.1875 to 0.1875
- narrow_basis: float32 [16, 256, 256], P('grp'), may hold values from -0.375 to 0.375
- wide_values: float32 [16, 1024], P('grp', 'wk'), may hold values from 0.001 to 0.1
- narrow_values: float32 [16, 256], P('grp'), may hold values from 0.001 to 0.1
Outputs:
- natural_grad: float32 [16, 1024, 256], P(None, 'wk')
The draws below stay inside these ranges and needn't reach their ends.
Inputs may be any that keep to these rules, and one draw needn't show every extreme that they name: `owned_layer`: every layer is owned by exactly one group.
All inputs are finite; a program needn't handle non-finite values.
Results may differ from the reference program's by a relative error of at most 0.0003.
Values may be sent and summed in bfloat16 or wider, within the bound.
No kernel may reach another device: no remote copies, remote signals or barrier semaphores. Data moves between devices by JAX's collectives and lax.ppermute only.
A program may use at most 128 MiB of HBM per device.

```python
import math
import jax
import jax.numpy as jnp
from jax import lax

WIDE = 1024
NARROW = 256
LAYERS = 16
TOKENS = 32768
N_GRP = 16


def spiked(drawn, stream_key, source, target, shards_of, factor):
    def block_of(dim):
        return (jnp.arange(drawn.shape[dim]) // (drawn.shape[dim] // shards_of)).reshape((-1,) + (1,) * (drawn.ndim - 1 - dim))

    first = jax.random.permutation(stream_key, shards_of)[block_of(target)]
    second = (block_of(target) + shards_of // 2) % shards_of
    return jnp.where((block_of(source) == first) | (block_of(source) == second), factor * drawn, drawn)


def block_levels(stream_key, extent, pieces, least, largest):
    def one(axis_at, blocks):
        heights = jax.random.uniform(jax.random.fold_in(jax.random.fold_in(stream_key, 6), axis_at), (blocks,), jnp.float32, least / len(pieces), largest / len(pieces))
        return jnp.repeat(jnp.exp(heights), extent[axis_at] // blocks).reshape((-1,) + (1,) * (len(extent) - axis_at - 1))

    factor_of = one(*pieces[0])
    for cut in pieces[1:]:
        factor_of = factor_of * one(*cut)
    return factor_of


def centred(rng, shape, spread, most, shards=(), held_as=jnp.bfloat16):
    values = jax.random.normal(rng, shape, jnp.float32) * spread
    if len(shards) > 0:
        values = block_levels(rng, shape, shards, -0.22, 0.18) * values
    return jnp.clip(values, min=-most, max=most).astype(held_as)


def gaussian_with(own_key, extent, scale, limit, cuts, heavy, dtype=jnp.bfloat16):
    drawn = scale * jax.random.normal(own_key, extent, jnp.float32)
    if cuts:
        drawn = drawn * block_levels(own_key, extent, cuts, -0.22, 0.18)
    return jnp.clip(spiked(drawn, jax.random.fold_in(own_key, 3), *heavy), -limit, limit).astype(dtype)


def setup_inputs(seed: int = 0) -> dict:
    keys = jax.random.split(jax.random.key(seed), 8)
    owned_layer = jax.random.permutation(keys[0], N_GRP).astype(jnp.int32)
    wide_side = gaussian_with(keys[1], (LAYERS, TOKENS, WIDE), 1.0, 24.0, ((1, 256),), (1, 2, 256, 6.0))
    narrow_side = centred(keys[2], (LAYERS, TOKENS, NARROW), 1.0, 6.0, ((1, 256),))
    wide_basis = centred(keys[3], (N_GRP, WIDE, WIDE), WIDE ** -0.5, 0.1875, ((0, 16), (1, 16)), jnp.float32)
    narrow_basis = centred(keys[4], (N_GRP, NARROW, NARROW), NARROW ** -0.5, 0.375, ((0, 16),), jnp.float32)
    wide_values = jnp.clip(jnp.exp(math.log(0.1) - 4.6051702 * jax.random.uniform(keys[5], (N_GRP, WIDE), jnp.float32) ** block_levels(keys[5], (N_GRP, WIDE), ((0, 16), (1, 16)), -0.2, 0.2)), 0.001, 0.1)
    narrow_values = jnp.clip(jnp.exp(math.log(0.1) - 4.6051702 * jax.random.uniform(keys[6], (N_GRP, NARROW), jnp.float32) ** block_levels(keys[6], (N_GRP, NARROW), ((0, 16),), -0.2, 0.2)), 0.001, 0.1)
    return dict(owned_layer=owned_layer, wide_side=wide_side, narrow_side=narrow_side, wide_basis=wide_basis, narrow_basis=narrow_basis, wide_values=wide_values, narrow_values=narrow_values)


DAMPING = 0.001


def layer_gradient(layer_pair):
    wide_rows, narrow_rows = layer_pair
    return jnp.dot(wide_rows.T, narrow_rows, preferred_element_type=jnp.float32)


def reference(owned_layer, wide_side, narrow_side, wide_basis, narrow_basis, wide_values, narrow_values):
    highest = lax.Precision.HIGHEST
    gradients = lax.map(layer_gradient, (wide_side, narrow_side)) / TOKENS

    def precondition(slot_data):
        basis_big, basis_small, values_big, values_small, layer_index = slot_data
        gradient = gradients[layer_index]
        rotated = jnp.dot(jnp.dot(basis_big.T, gradient, precision=highest), basis_small, precision=highest)
        scaled = rotated / (values_big[:, None] * values_small[None, :] + DAMPING)
        returned = jnp.dot(scaled, basis_small.T, precision=highest)
        return jnp.dot(basis_big, returned, precision=highest)

    slot_results = lax.map(precondition, (wide_basis, narrow_basis, wide_values, narrow_values, owned_layer))
    return jnp.zeros_like(slot_results).at[owned_layer].set(slot_results)
```

```python
import jax
import jax.numpy as jnp
from jax import lax
from jax.experimental import pallas as pl
from jax.experimental.pallas import tpu as pltpu
from jax.sharding import Mesh, PartitionSpec as P

DAMPING = 0.001
GRP = ("x", "yl", "core")
WK = ("z", "yh")
HIGH = lax.Precision.HIGH


def pack_kernel(owned_ref, wide_ref, narrow_ref, out_ref):
    wide = wide_ref.shape[2]
    out_ref[:, :, :wide] = wide_ref[...]
    out_ref[:, :, wide:] = narrow_ref[...]


def pack_tokens(owned_layer, wide_side, narrow_side):
    layers, tokens, wide = wide_side.shape
    narrow = narrow_side.shape[2]
    return pl.pallas_call(
        pack_kernel,
        out_shape=jax.ShapeDtypeStruct((layers, tokens, wide + narrow), wide_side.dtype),
        grid_spec=pltpu.PrefetchScalarGridSpec(
            num_scalar_prefetch=1,
            grid=(layers,),
            in_specs=[
                pl.BlockSpec((1, tokens, wide), lambda i, owned: (owned[i], 0, 0)),
                pl.BlockSpec((1, tokens, narrow), lambda i, owned: (owned[i], 0, 0)),
            ],
            out_specs=pl.BlockSpec((1, tokens, wide + narrow), lambda i, owned: (i, 0, 0)),
        ),
    )(owned_layer, wide_side, narrow_side)


def local(
    owned_layer, wide_side, narrow_side, wide_basis, narrow_basis, wide_values, narrow_values
):
    groups = lax.axis_size(GRP)
    workers = lax.axis_size(WK)
    layers, tokens, wide = wide_side.shape
    narrow = narrow_side.shape[2]
    total_tokens = tokens * groups * workers
    rows = wide // workers
    cols = narrow // workers

    values_row = jnp.pad(wide_values, ((0, 7), (0, wide - rows)))
    held = jnp.concatenate([wide_basis[0], values_row], axis=0)
    held = lax.all_gather(held, "yh", axis=0, tiled=False)
    held = lax.all_gather(held, "z", axis=0, tiled=False)
    held = held.reshape(workers, rows + 8, wide)
    basis = held[:, :rows].reshape(wide, wide)
    wide_all = held[:, rows, :rows].reshape(wide)

    packed = pack_tokens(owned_layer, wide_side, narrow_side)
    packed = lax.all_to_all(packed, GRP, 0, 0, tiled=True)
    packed = packed.reshape(groups * tokens, wide + narrow)
    partial = lax.dot_general(
        packed[:, wide:], packed[:, :wide], (((0,), (0,)), ((), ())),
        preferred_element_type=jnp.float32,
    )
    small = narrow_basis[0]
    partial = lax.dot_general(small, partial, (((0,), (0,)), ((), ())), precision=HIGH)
    partial = lax.all_to_all(partial.reshape(workers, cols, wide), WK, 0, 0, tiled=True)
    gradient = jnp.sum(partial, axis=0) / total_tokens
    rotated = jnp.dot(gradient, basis, precision=HIGH)
    worker = lax.axis_index(WK)
    values_small = lax.dynamic_slice(narrow_values[0], (worker * cols,), (cols,))
    scaled = rotated / (values_small[:, None] * wide_all[None, :] + DAMPING)
    precond = lax.dot_general(scaled, basis, (((1,), (1,)), ((), ())), precision=HIGH)
    precond = precond.reshape(cols, workers, rows).transpose(1, 0, 2)
    precond = lax.all_to_all(precond, WK, 0, 0, tiled=True).reshape(narrow, rows)
    mine = lax.dot_general(precond, small, (((0,), (1,)), ((), ())), precision=HIGH)
    gathered = lax.all_gather(mine, GRP, axis=0, tiled=False)
    return jnp.zeros_like(gathered).at[owned_layer].set(gathered)


def solution(mesh):
    fine = Mesh(
        mesh.devices.reshape(4, 2, 2, 8, 2), ("x", "yl", "core", "z", "yh")
    )
    return jax.shard_map(
        local,
        mesh=fine,
        in_specs=(
            P(),
            P(None, GRP + WK, None),
            P(None, GRP + WK, None),
            P(GRP, WK, None),
            P(GRP, None, None),
            P(GRP, WK),
            P(GRP, None),
        ),
        out_specs=P(None, WK, None),
        check_vma=False,
    )
```

```python
import jax
import jax.numpy as jnp
from jax import lax
from jax.experimental import pallas as pl
from jax.experimental.pallas import tpu as pltpu
from jax.sharding import Mesh, PartitionSpec as P

DAMPING = 0.001
GRP = ("x", "yl", "core")
WK = ("z", "yh")
HIGH = lax.Precision.HIGH
PACK_SPACE = pltpu.VMEM


def pack_kernel(owned_ref, wide_ref, narrow_ref, out_ref, sems):
    layers, _, wide = wide_ref.shape
    narrow = narrow_ref.shape[2]
    copies = []
    for group in range(layers):
        layer = owned_ref[group]
        copies.append(
            pltpu.make_async_copy(
                wide_ref.at[layer], out_ref.at[group, :, pl.ds(0, wide)], sems.at[group, 0]
            )
        )
        copies.append(
            pltpu.make_async_copy(
                narrow_ref.at[layer], out_ref.at[group, :, pl.ds(wide, narrow)], sems.at[group, 1]
            )
        )
    for copy in copies:
        copy.start()
    for copy in copies:
        copy.wait()


def pack_tokens(owned_layer, wide_side, narrow_side):
    layers, tokens, wide = wide_side.shape
    narrow = narrow_side.shape[2]
    return pl.pallas_call(
        pack_kernel,
        out_shape=jax.ShapeDtypeStruct((layers, tokens, wide + narrow), wide_side.dtype),
        in_specs=[
            pl.BlockSpec(memory_space=pltpu.SMEM),
            pl.BlockSpec(memory_space=pl.ANY),
            pl.BlockSpec(memory_space=pl.ANY),
        ],
        out_specs=pl.BlockSpec(memory_space=PACK_SPACE),
        scratch_shapes=[pltpu.SemaphoreType.DMA((layers, 2))],
    )(owned_layer, wide_side, narrow_side)


def place_kernel(owned_ref, core_ref, mine_ref, other_ref, out_ref, sems):
    core = core_ref[0]
    chips = mine_ref.shape[0]
    copies = []
    for chip in range(chips):
        copies.append(
            pltpu.make_async_copy(
                mine_ref.at[chip], out_ref.at[owned_ref[2 * chip + core]], sems.at[chip, 0]
            )
        )
        copies.append(
            pltpu.make_async_copy(
                other_ref.at[chip], out_ref.at[owned_ref[2 * chip + 1 - core]], sems.at[chip, 1]
            )
        )
    for copy in copies:
        copy.start()
    for copy in copies:
        copy.wait()


def place(owned_layer, core, mine, other):
    chips, rows, narrow = mine.shape
    return pl.pallas_call(
        place_kernel,
        out_shape=jax.ShapeDtypeStruct((2 * chips, rows, narrow), mine.dtype),
        in_specs=[
            pl.BlockSpec(memory_space=pltpu.SMEM),
            pl.BlockSpec(memory_space=pltpu.SMEM),
            pl.BlockSpec(memory_space=pltpu.VMEM),
            pl.BlockSpec(memory_space=pltpu.VMEM),
        ],
        out_specs=pl.BlockSpec(memory_space=pl.ANY),
        scratch_shapes=[pltpu.SemaphoreType.DMA((chips, 2))],
    )(owned_layer, core, mine, other)


def local(
    owned_layer, wide_side, narrow_side, wide_basis, narrow_basis, wide_values, narrow_values
):
    groups = lax.axis_size(GRP)
    workers = lax.axis_size(WK)
    layers, tokens, wide = wide_side.shape
    narrow = narrow_side.shape[2]
    total_tokens = tokens * groups * workers
    rows = wide // workers
    cols = narrow // workers

    packed = pack_tokens(owned_layer, wide_side, narrow_side)
    values_row = jnp.pad(wide_values, ((0, 7), (0, wide - rows)))
    held = jnp.concatenate([wide_basis[0], values_row], axis=0)
    swapped = lax.ppermute(held, "yh", [(0, 1), (1, 0)])
    low = lax.axis_index("yh") == 0
    held = jnp.stack([jnp.where(low, held, swapped), jnp.where(low, swapped, held)])
    worker = lax.axis_index(WK)
    values_small = lax.dynamic_slice(narrow_values[0], (worker * cols,), (cols,))
    held, packed, values_small = lax.optimization_barrier((held, packed, values_small))
    held = lax.all_gather(held, "z", axis=0, tiled=False)
    held = held.reshape(workers, rows + 8, wide)
    basis = held[:, :rows].reshape(wide, wide)
    wide_all = held[:, rows, :rows].reshape(wide)

    packed = lax.all_to_all(packed, GRP, 0, 0, tiled=True)
    packed = packed.reshape(groups * tokens, wide + narrow)
    partial = lax.dot_general(
        packed[:, wide:], packed[:, :wide], (((0,), (0,)), ((), ())),
        preferred_element_type=jnp.float32,
    )
    small = narrow_basis[0]
    partial = lax.dot_general(small, partial, (((0,), (0,)), ((), ())), precision=HIGH)
    partial = lax.all_to_all(partial.reshape(workers, cols, wide), WK, 0, 0, tiled=True)
    gradient = jnp.sum(partial, axis=0) / total_tokens
    rotated = jnp.dot(gradient, basis, precision=HIGH)
    scaled = rotated / (values_small[:, None] * wide_all[None, :] + DAMPING)
    precond = lax.dot_general(scaled, basis, (((1,), (1,)), ((), ())), precision=HIGH)
    precond = precond.reshape(cols, workers, rows).transpose(1, 0, 2)
    precond = lax.all_to_all(precond, WK, 0, 0, tiled=True).reshape(narrow, rows)
    mine = lax.dot_general(precond, small, (((0,), (1,)), ((), ())), precision=HIGH)
    spread = jnp.broadcast_to(mine[None], (groups // 2,) + mine.shape)
    spread = lax.all_to_all(spread, ("x", "yl"), 0, 0, tiled=True)
    other = lax.ppermute(spread, "core", [(0, 1), (1, 0)])
    return place(owned_layer, lax.axis_index("core").reshape(1), spread, other)


def solution(mesh):
    fine = Mesh(
        mesh.devices.reshape(4, 2, 2, 8, 2), ("x", "yl", "core", "z", "yh")
    )
    return jax.shard_map(
        local,
        mesh=fine,
        in_specs=(
            P(),
            P(None, GRP + WK, None),
            P(None, GRP + WK, None),
            P(GRP, WK, None),
            P(GRP, None, None),
            P(GRP, WK),
            P(GRP, None),
        ),
        out_specs=P(None, WK, None),
        check_vma=False,
    )
```

```python
import functools

import jax
import jax.numpy as jnp
from jax import lax
from jax.experimental import pallas as pl
from jax.experimental.pallas import tpu as pltpu
from jax.sharding import Mesh, PartitionSpec as P

DAMPING = 0.001
LIMIT = float(2**17 - 2)
VALUE_UNIT = float(2**33)
GRP = ("x", "yl", "core")
WK = ("z", "yh")
HIGH = lax.Precision.HIGH
PACK_GRANT = 59 * 2**20
MIDDLE_GRANT = 24 * 2**20
ENCODE_GRANT = 24 * 2**20


def pack_kernel(owned_ref, wide_ref, narrow_ref, out_ref, stage_ref, load_sems, store_sems):
    layers, _, wide = wide_ref.shape
    narrow = narrow_ref.shape[2]
    loads, stores = [], []
    for group in range(layers):
        layer = owned_ref[group]
        stage = stage_ref.at[group]
        loads.append(
            (
                pltpu.make_async_copy(
                    wide_ref.at[layer], stage.at[:, pl.ds(0, wide)], load_sems.at[group, 0]
                ),
                pltpu.make_async_copy(
                    narrow_ref.at[layer], stage.at[:, pl.ds(wide, narrow)], load_sems.at[group, 1]
                ),
            )
        )
        stores.append(pltpu.make_async_copy(stage, out_ref.at[group], store_sems.at[group]))
    for pair in loads:
        pair[0].start()
        pair[1].start()
    for pair, store in zip(loads, stores):
        pair[0].wait()
        pair[1].wait()
        store.start()
    for store in stores:
        store.wait()


def pack_tokens(owned_layer, wide_side, narrow_side):
    layers, tokens, wide = wide_side.shape
    narrow = narrow_side.shape[2]
    packed = (layers, tokens, wide + narrow)
    return pl.pallas_call(
        pack_kernel,
        out_shape=jax.ShapeDtypeStruct(packed, wide_side.dtype),
        in_specs=[
            pl.BlockSpec(memory_space=pltpu.SMEM),
            pl.BlockSpec(memory_space=pl.ANY),
            pl.BlockSpec(memory_space=pl.ANY),
        ],
        out_specs=pl.BlockSpec(memory_space=pl.ANY),
        scratch_shapes=[
            pltpu.VMEM(packed, wide_side.dtype),
            pltpu.SemaphoreType.DMA((layers, 2)),
            pltpu.SemaphoreType.DMA((layers,)),
        ],
        compiler_params=pltpu.CompilerParams(vmem_limit_bytes=PACK_GRANT),
    )(owned_layer, wide_side, narrow_side)


def place_kernel(owned_ref, core_ref, mine_ref, other_ref, out_ref, sems):
    core = core_ref[0]
    chips = mine_ref.shape[0]
    copies = []
    for chip in range(chips):
        copies.append(
            pltpu.make_async_copy(
                mine_ref.at[chip], out_ref.at[owned_ref[2 * chip + core]], sems.at[chip, 0]
            )
        )
        copies.append(
            pltpu.make_async_copy(
                other_ref.at[chip], out_ref.at[owned_ref[2 * chip + 1 - core]], sems.at[chip, 1]
            )
        )
    for copy in copies:
        copy.start()
    for copy in copies:
        copy.wait()


def place(owned_layer, core, mine, other):
    chips, rows, narrow = mine.shape
    return pl.pallas_call(
        place_kernel,
        out_shape=jax.ShapeDtypeStruct((2 * chips, rows, narrow), mine.dtype),
        in_specs=[
            pl.BlockSpec(memory_space=pltpu.SMEM),
            pl.BlockSpec(memory_space=pltpu.SMEM),
            pl.BlockSpec(memory_space=pltpu.VMEM),
            pl.BlockSpec(memory_space=pltpu.VMEM),
        ],
        out_specs=pl.BlockSpec(memory_space=pl.ANY),
        scratch_shapes=[pltpu.SemaphoreType.DMA((chips, 2))],
        compiler_params=pltpu.CompilerParams(vmem_limit_bytes=4 * 2**20),
    )(owned_layer, core, mine, other)


def split(value):
    high = value.astype(jnp.bfloat16)
    return high, (value - high.astype(jnp.float32)).astype(jnp.bfloat16)


def product(value, high, low, contract):
    rows = value.shape[0]
    dims = (((1,), (contract,)), ((), ()))
    value_high, value_low = split(value)
    both = lax.dot_general(
        jnp.concatenate([value_high, value_low], axis=0), high, dims,
        preferred_element_type=jnp.float32,
    )
    rest = lax.dot_general(value_high, low, dims, preferred_element_type=jnp.float32)
    return both[:rows] + both[rows:] + rest


def encode_kernel(sums_ref, small_ref, values_ref, held_ref, out_ref, basis_ref, sem):
    load = pltpu.make_async_copy(held_ref, basis_ref, sem)
    load.start()
    workers = out_ref.shape[0]
    narrow = small_ref.shape[1]
    rows = narrow // workers
    half = rows // 2
    tiles = sums_ref.shape[1] // 128
    base = tiles * half
    lane = lax.broadcasted_iota(jnp.int32, (half, 128), 1)
    values = (values_ref[...] * VALUE_UNIT).astype(jnp.int32)
    values = jnp.concatenate([values, jnp.zeros_like(values)], axis=1)
    values = jnp.broadcast_to(values, (half, 128))
    high, low_part = split(sums_ref[...])
    parts = product(small_ref[0].T, high, low_part, 0)
    for worker in range(workers):
        part = parts[worker * rows : (worker + 1) * rows, :]
        most = jnp.max(jnp.abs(part), axis=1, keepdims=True)
        power = jnp.ceil(jnp.log2(jnp.maximum(most, 2.0**-125)))
        code = jnp.floor(part * (jnp.exp2(-power) * LIMIT) + 0.5).astype(jnp.int32)
        low = jnp.zeros((half, 128), jnp.int32)
        for tile in range(tiles):
            piece = code[:, tile * 128 : (tile + 1) * 128]
            first, second = piece[:half], piece[half:]
            out_ref[worker, tile * half : (tile + 1) * half, :] = ((first >> 2) << 16) | (
                (second >> 2) & 0xFFFF
            )
            low = low | ((first & 3) << (4 * tile)) | ((second & 3) << (4 * tile + 2))
        out_ref[worker, base : base + half, :] = low
        power = power.astype(jnp.int32)
        out_ref[worker, base + half :, :] = jnp.where(
            lane < 64, values, jnp.where(lane < 96, power[:half], power[half:])
        )
    load.wait()


def encode(sums, narrow_basis, wide_values, held, workers):
    narrow, wide = sums.shape
    words = (narrow // workers // 2) * (wide // 128 + 2)
    return pl.pallas_call(
        encode_kernel,
        out_shape=(
            jax.ShapeDtypeStruct((workers, words, 128), jnp.int32),
            jax.ShapeDtypeStruct(held.shape, held.dtype),
        ),
        in_specs=[pl.BlockSpec(memory_space=pltpu.VMEM)] * 3 + [pl.BlockSpec(memory_space=pl.ANY)],
        out_specs=(pl.BlockSpec(memory_space=pltpu.VMEM), pl.BlockSpec(memory_space=pltpu.VMEM)),
        scratch_shapes=[pltpu.SemaphoreType.DMA],
        compiler_params=pltpu.CompilerParams(vmem_limit_bytes=ENCODE_GRANT),
    )(sums, narrow_basis, wide_values, held)


def middle_kernel(total_tokens, worker_ref, coded_ref, basis_ref, small_ref, out_ref):
    workers, words, _ = coded_ref.shape
    half = 8
    tiles = words // half - 2
    base = tiles * half
    lane = lax.broadcasted_iota(jnp.int32, (half, 128), 1)
    sums = [[jnp.zeros((half, 128), jnp.float32) for _ in range(tiles)] for _ in range(2)]
    values = []
    for worker in range(workers):
        tail = coded_ref[worker, base + half :, :]
        values.append(tail.astype(jnp.float32) * (1.0 / VALUE_UNIT))
        units = [
            jnp.exp2(tail[:, at : at + 1].astype(jnp.float32)) * (1.0 / LIMIT) for at in (64, 96)
        ]
        low = coded_ref[worker, base : base + half, :]
        for tile in range(tiles):
            word = coded_ref[worker, tile * half : (tile + 1) * half, :]
            first = ((word >> 16) << 2) | ((low >> (4 * tile)) & 3)
            second = (((word << 16) >> 16) << 2) | ((low >> (4 * tile + 2)) & 3)
            sums[0][tile] += first.astype(jnp.float32) * units[0]
            sums[1][tile] += second.astype(jnp.float32) * units[1]
    gradient = jnp.concatenate(
        [jnp.concatenate(part, axis=1) for part in sums], axis=0
    ) * (1.0 / total_tokens)
    wide_values = jnp.concatenate(
        [
            jnp.where(lane < 64, values[2 * tile], pltpu.roll(values[2 * tile + 1], 64, 1))
            for tile in range(tiles)
        ],
        axis=1,
    )[:1]
    count = small_ref.shape[1]
    own = lax.broadcasted_iota(jnp.int32, (2 * half, count), 1) == (
        worker_ref[0] * (2 * half) + lax.broadcasted_iota(jnp.int32, (2 * half, count), 0)
    )
    small = jnp.sum(jnp.where(own, small_ref[...], 0.0), axis=1, keepdims=True)
    high, low = (
        jnp.concatenate(
            [basis_ref[z, h, i] for z in range(basis_ref.shape[0]) for h in range(basis_ref.shape[1])],
            axis=0,
        )
        for i in range(2)
    )
    rotated = product(gradient, high, low, 0)
    scaled = rotated / (small * wide_values + DAMPING)
    precond = product(scaled, high, low, 1)
    for tile in range(tiles):
        piece = precond[:, tile * 128 : (tile + 1) * 128]
        first, second = piece[:half], piece[half:]
        out_ref[2 * tile] = jnp.where(lane < 64, first, pltpu.roll(second, 64, 1))
        out_ref[2 * tile + 1] = jnp.where(lane < 64, pltpu.roll(first, 64, 1), second)


def middle(worker, coded, basis, narrow_values, total_tokens):
    return pl.pallas_call(
        functools.partial(middle_kernel, total_tokens),
        out_shape=jax.ShapeDtypeStruct((coded.shape[0], 8, 128), jnp.float32),
        in_specs=[pl.BlockSpec(memory_space=pltpu.SMEM)] + [pl.BlockSpec(memory_space=pltpu.VMEM)] * 3,
        out_specs=pl.BlockSpec(memory_space=pltpu.VMEM),
        compiler_params=pltpu.CompilerParams(vmem_limit_bytes=MIDDLE_GRANT),
    )(worker, coded, basis, narrow_values)


def last_kernel(precond_ref, small_ref, out_ref):
    pieces = []
    for worker in range(precond_ref.shape[0]):
        block = precond_ref[worker]
        pieces += [block[:, :64], block[:, 64:]]
    columns = jnp.concatenate(pieces, axis=0)
    mine = lax.dot_general(
        columns.T, small_ref[0], (((1,), (1,)), ((), ())),
        precision=lax.Precision.HIGHEST, preferred_element_type=jnp.float32,
    )
    for chip in range(out_ref.shape[0]):
        out_ref[chip] = mine


def last(precond, narrow_basis, chips):
    return pl.pallas_call(
        last_kernel,
        out_shape=jax.ShapeDtypeStruct((chips, 64, narrow_basis.shape[1]), jnp.float32),
        in_specs=[pl.BlockSpec(memory_space=pltpu.VMEM)] * 2,
        out_specs=pl.BlockSpec(memory_space=pltpu.VMEM),
        compiler_params=pltpu.CompilerParams(vmem_limit_bytes=4 * 2**20),
    )(precond, narrow_basis)


def local(
    owned_layer, wide_side, narrow_side, wide_basis, narrow_basis, wide_values, narrow_values
):
    groups = lax.axis_size(GRP)
    workers = lax.axis_size(WK)
    layers, tokens, wide = wide_side.shape
    narrow = narrow_side.shape[2]
    total_tokens = tokens * groups * workers

    swapped = lax.ppermute(wide_basis[0], "yh", [(0, 1), (1, 0)])
    packed = pack_tokens(owned_layer, wide_side, narrow_side)
    low = lax.axis_index("yh") == 0
    held = jnp.stack(
        [jnp.where(low, wide_basis[0], swapped), jnp.where(low, swapped, wide_basis[0])]
    )
    high = lax.reduce_precision(held, 8, 7)
    held = jnp.stack([high.astype(jnp.bfloat16), (held - high).astype(jnp.bfloat16)], axis=1)
    worker = lax.axis_index(WK).reshape(1)
    core = lax.axis_index("core").reshape(1)
    held, packed, worker, core = lax.optimization_barrier((held, packed, worker, core))
    held = lax.all_gather(held, "z", axis=0, tiled=False)

    packed = lax.all_to_all(packed, GRP, 0, 0, tiled=True)
    packed = packed.reshape(groups * tokens, wide + narrow)
    sums = lax.dot_general(
        packed[:, wide:], packed[:, :wide], (((0,), (0,)), ((), ())),
        preferred_element_type=jnp.float32,
    )
    coded, basis = encode(sums, narrow_basis, wide_values, held, workers)
    coded = lax.all_to_all(coded, WK, 0, 0, tiled=True)
    precond = middle(worker, coded, basis, narrow_values, total_tokens)
    precond = lax.all_to_all(precond, WK, 0, 0, tiled=True)
    spread = last(precond, narrow_basis, groups // 2)
    spread = lax.all_to_all(spread, ("x", "yl"), 0, 0, tiled=True)
    other = lax.ppermute(spread, "core", [(0, 1), (1, 0)])
    return place(owned_layer, core, spread, other)


def solution(mesh):
    fine = Mesh(
        mesh.devices.reshape(4, 2, 2, 8, 2), ("x", "yl", "core", "z", "yh")
    )
    return jax.shard_map(
        local,
        mesh=fine,
        in_specs=(
            P(),
            P(None, GRP + WK, None),
            P(None, GRP + WK, None),
            P(GRP, WK, None),
            P(GRP, None, None),
            P(GRP, WK),
            P(GRP, None),
        ),
        out_specs=P(None, WK, None),
        check_vma=False,
    )
```

```python
import functools

import jax
import jax.numpy as jnp
from jax import lax
from jax.experimental import pallas as pl
from jax.experimental.pallas import tpu as pltpu
from jax.sharding import Mesh, PartitionSpec as P

DAMPING = 0.001
LIMIT = float(2**17 - 2)
VALUE_UNIT = float(2**33)
GRP = ("x", "yl", "core")
WK = ("z", "yh")
HIGH = lax.Precision.HIGH
PLACE_GRANT = 4 * 2**20
PACK_GRANT = 59 * 2**20
MIDDLE_GRANT = 24 * 2**20
ENCODE_GRANT = 47 * 2**20


def pack_kernel(owned_ref, wide_ref, narrow_ref, out_ref, stage_ref, load_sems, store_sems):
    layers, _, wide = wide_ref.shape
    narrow = narrow_ref.shape[2]
    loads, stores = [], []
    for group in range(layers):
        layer = owned_ref[group]
        stage = stage_ref.at[group]
        loads.append(
            (
                pltpu.make_async_copy(
                    wide_ref.at[layer], stage.at[:, pl.ds(0, wide)], load_sems.at[group, 0]
                ),
                pltpu.make_async_copy(
                    narrow_ref.at[layer], stage.at[:, pl.ds(wide, narrow)], load_sems.at[group, 1]
                ),
            )
        )
        stores.append(pltpu.make_async_copy(stage, out_ref.at[group], store_sems.at[group]))
    for pair in loads:
        pair[0].start()
        pair[1].start()
    for pair, store in zip(loads, stores):
        pair[0].wait()
        pair[1].wait()
        store.start()
    for store in stores:
        store.wait()


def pack_tokens(owned_layer, wide_side, narrow_side):
    layers, tokens, wide = wide_side.shape
    narrow = narrow_side.shape[2]
    packed = (layers, tokens, wide + narrow)
    return pl.pallas_call(
        pack_kernel,
        out_shape=jax.ShapeDtypeStruct(packed, wide_side.dtype),
        in_specs=[
            pl.BlockSpec(memory_space=pltpu.SMEM),
            pl.BlockSpec(memory_space=pl.ANY),
            pl.BlockSpec(memory_space=pl.ANY),
        ],
        out_specs=pl.BlockSpec(memory_space=pl.ANY),
        scratch_shapes=[
            pltpu.VMEM(packed, wide_side.dtype),
            pltpu.SemaphoreType.DMA((layers, 2)),
            pltpu.SemaphoreType.DMA((layers,)),
        ],
        compiler_params=pltpu.CompilerParams(vmem_limit_bytes=PACK_GRANT),
    )(owned_layer, wide_side, narrow_side)


def place_kernel(owned_ref, which_ref, blocks_ref, *rest):
    out_ref, sems = rest[-2:]
    which = which_ref[0]
    copies = [
        pltpu.make_async_copy(
            blocks_ref.at[chip], out_ref.at[owned_ref[2 * chip + which]], sems.at[chip]
        )
        for chip in range(blocks_ref.shape[0])
    ]
    for copy in copies:
        copy.start()
    for copy in copies:
        copy.wait()


def place(owned_layer, which, blocks, into=None):
    chips, rows, narrow = blocks.shape
    more = () if into is None else (into,)
    return pl.pallas_call(
        place_kernel,
        out_shape=jax.ShapeDtypeStruct((2 * chips, rows, narrow), blocks.dtype),
        in_specs=[
            pl.BlockSpec(memory_space=pltpu.SMEM),
            pl.BlockSpec(memory_space=pltpu.SMEM),
            pl.BlockSpec(memory_space=pltpu.VMEM),
        ]
        + [pl.BlockSpec(memory_space=pl.ANY)] * len(more),
        out_specs=pl.BlockSpec(memory_space=pl.ANY),
        input_output_aliases={3: 0} if more else {},
        scratch_shapes=[pltpu.SemaphoreType.DMA((chips,))],
        compiler_params=pltpu.CompilerParams(vmem_limit_bytes=PLACE_GRANT),
    )(owned_layer, which, blocks, *more)


def split(value):
    high = value.astype(jnp.bfloat16)
    return high, (value - high.astype(jnp.float32)).astype(jnp.bfloat16)


def product(value, high, low, contract):
    rows = value.shape[0]
    dims = (((1,), (contract,)), ((), ()))
    value_high, value_low = split(value)
    both = lax.dot_general(
        jnp.concatenate([value_high, value_low], axis=0), high, dims,
        preferred_element_type=jnp.float32,
    )
    rest = lax.dot_general(value_high, low, dims, preferred_element_type=jnp.float32)
    return both[:rows] + both[rows:] + rest


def encode_kernel(sums_ref, small_ref, values_ref, held_ref, out_ref, basis_ref, sems):
    loads = [
        pltpu.make_async_copy(held_ref.at[z], basis_ref.at[z], sems.at[z])
        for z in range(held_ref.shape[0])
    ]
    for load in loads:
        load.start()
    workers = out_ref.shape[0]
    narrow = small_ref.shape[1]
    rows = narrow // workers
    half = rows // 2
    tiles = sums_ref.shape[1] // 128
    base = tiles * half
    lane = lax.broadcasted_iota(jnp.int32, (half, 128), 1)
    values = (values_ref[...] * VALUE_UNIT).astype(jnp.int32)
    values = jnp.concatenate([values, jnp.zeros_like(values)], axis=1)
    values = jnp.broadcast_to(values, (half, 128))
    high, low_part = split(sums_ref[...])
    parts = product(small_ref[0].T, high, low_part, 0)
    for worker in range(workers):
        part = parts[worker * rows : (worker + 1) * rows, :]
        most = jnp.max(jnp.abs(part), axis=1, keepdims=True)
        power = jnp.ceil(jnp.log2(jnp.maximum(most, 2.0**-125)))
        code = jnp.floor(part * (jnp.exp2(-power) * LIMIT) + 0.5).astype(jnp.int32)
        low = jnp.zeros((half, 128), jnp.int32)
        for tile in range(tiles):
            piece = code[:, tile * 128 : (tile + 1) * 128]
            first, second = piece[:half], piece[half:]
            out_ref[worker, tile * half : (tile + 1) * half, :] = ((first >> 2) << 16) | (
                (second >> 2) & 0xFFFF
            )
            low = low | ((first & 3) << (4 * tile)) | ((second & 3) << (4 * tile + 2))
        out_ref[worker, base : base + half, :] = low
        power = power.astype(jnp.int32)
        out_ref[worker, base + half :, :] = jnp.where(
            lane < 64, values, jnp.where(lane < 96, power[:half], power[half:])
        )
    for load in loads:
        load.wait()


def encode(sums, narrow_basis, wide_values, held, workers):
    narrow, wide = sums.shape
    words = (narrow // workers // 2) * (wide // 128 + 2)
    return pl.pallas_call(
        encode_kernel,
        out_shape=(
            jax.ShapeDtypeStruct((workers, words, 128), jnp.int32),
            jax.ShapeDtypeStruct(held.shape, held.dtype),
        ),
        in_specs=[pl.BlockSpec(memory_space=pltpu.VMEM)] * 3 + [pl.BlockSpec(memory_space=pl.ANY)],
        out_specs=(pl.BlockSpec(memory_space=pltpu.VMEM), pl.BlockSpec(memory_space=pltpu.VMEM)),
        scratch_shapes=[pltpu.SemaphoreType.DMA((held.shape[0],))],
        compiler_params=pltpu.CompilerParams(vmem_limit_bytes=ENCODE_GRANT),
    )(sums, narrow_basis, wide_values, held)


def middle_kernel(total_tokens, worker_ref, coded_ref, basis_ref, small_ref, out_ref):
    workers, words, _ = coded_ref.shape
    half = 8
    tiles = words // half - 2
    base = tiles * half
    lane = lax.broadcasted_iota(jnp.int32, (half, 128), 1)
    sums = [[jnp.zeros((half, 128), jnp.float32) for _ in range(tiles)] for _ in range(2)]
    values = []
    for worker in range(workers):
        tail = coded_ref[worker, base + half :, :]
        values.append(tail.astype(jnp.float32) * (1.0 / VALUE_UNIT))
        units = [
            jnp.exp2(tail[:, at : at + 1].astype(jnp.float32)) * (1.0 / LIMIT) for at in (64, 96)
        ]
        low = coded_ref[worker, base : base + half, :]
        for tile in range(tiles):
            word = coded_ref[worker, tile * half : (tile + 1) * half, :]
            first = ((word >> 16) << 2) | ((low >> (4 * tile)) & 3)
            second = (((word << 16) >> 16) << 2) | ((low >> (4 * tile + 2)) & 3)
            sums[0][tile] += first.astype(jnp.float32) * units[0]
            sums[1][tile] += second.astype(jnp.float32) * units[1]
    gradient = jnp.concatenate(
        [jnp.concatenate(part, axis=1) for part in sums], axis=0
    ) * (1.0 / total_tokens)
    wide_values = jnp.concatenate(
        [
            jnp.where(lane < 64, values[2 * tile], pltpu.roll(values[2 * tile + 1], 64, 1))
            for tile in range(tiles)
        ],
        axis=1,
    )[:1]
    count = small_ref.shape[1]
    own = lax.broadcasted_iota(jnp.int32, (2 * half, count), 1) == (
        worker_ref[0] * (2 * half) + lax.broadcasted_iota(jnp.int32, (2 * half, count), 0)
    )
    small = jnp.sum(jnp.where(own, small_ref[...], 0.0), axis=1, keepdims=True)
    high, low = (
        jnp.concatenate(
            [basis_ref[z, h, i] for z in range(basis_ref.shape[0]) for h in range(basis_ref.shape[1])],
            axis=0,
        )
        for i in range(2)
    )
    rotated = product(gradient, high, low, 0)
    scaled = rotated / (small * wide_values + DAMPING)
    precond = product(scaled, high, low, 1)
    for tile in range(tiles):
        piece = precond[:, tile * 128 : (tile + 1) * 128]
        first, second = piece[:half], piece[half:]
        out_ref[2 * tile] = jnp.where(lane < 64, first, pltpu.roll(second, 64, 1))
        out_ref[2 * tile + 1] = jnp.where(lane < 64, pltpu.roll(first, 64, 1), second)


def middle(worker, coded, basis, narrow_values, total_tokens):
    return pl.pallas_call(
        functools.partial(middle_kernel, total_tokens),
        out_shape=jax.ShapeDtypeStruct((coded.shape[0], 8, 128), jnp.float32),
        in_specs=[pl.BlockSpec(memory_space=pltpu.SMEM)] + [pl.BlockSpec(memory_space=pltpu.VMEM)] * 3,
        out_specs=pl.BlockSpec(memory_space=pltpu.VMEM),
        compiler_params=pltpu.CompilerParams(vmem_limit_bytes=MIDDLE_GRANT),
    )(worker, coded, basis, narrow_values)


def last_kernel(precond_ref, small_ref, out_ref):
    pieces = []
    for worker in range(precond_ref.shape[0]):
        block = precond_ref[worker]
        pieces += [block[:, :64], block[:, 64:]]
    columns = jnp.concatenate(pieces, axis=0)
    mine = lax.dot_general(
        columns.T, small_ref[0], (((1,), (1,)), ((), ())),
        precision=lax.Precision.HIGHEST, preferred_element_type=jnp.float32,
    )
    for chip in range(out_ref.shape[0]):
        out_ref[chip] = mine


def last(precond, narrow_basis, chips):
    return pl.pallas_call(
        last_kernel,
        out_shape=jax.ShapeDtypeStruct((chips, 64, narrow_basis.shape[1]), jnp.float32),
        in_specs=[pl.BlockSpec(memory_space=pltpu.VMEM)] * 2,
        out_specs=pl.BlockSpec(memory_space=pltpu.VMEM),
        compiler_params=pltpu.CompilerParams(vmem_limit_bytes=4 * 2**20),
    )(precond, narrow_basis)


def local(
    owned_layer, wide_side, narrow_side, wide_basis, narrow_basis, wide_values, narrow_values
):
    groups = lax.axis_size(GRP)
    workers = lax.axis_size(WK)
    layers, tokens, wide = wide_side.shape
    narrow = narrow_side.shape[2]
    total_tokens = tokens * groups * workers

    swapped = lax.ppermute(wide_basis[0], "yh", [(0, 1), (1, 0)])
    packed = pack_tokens(owned_layer, wide_side, narrow_side)
    low = lax.axis_index("yh") == 0
    held = jnp.stack(
        [jnp.where(low, wide_basis[0], swapped), jnp.where(low, swapped, wide_basis[0])]
    )
    high = lax.reduce_precision(held, 8, 7)
    held = jnp.stack([high.astype(jnp.bfloat16), (held - high).astype(jnp.bfloat16)], axis=1)
    worker = lax.axis_index(WK).reshape(1)
    core = lax.axis_index("core").reshape(1)
    held, packed, worker, core = lax.optimization_barrier((held, packed, worker, core))
    held = lax.all_gather(held, "z", axis=0, tiled=False)

    packed = lax.all_to_all(packed, GRP, 0, 0, tiled=True)
    packed = packed.reshape(groups * tokens, wide + narrow)
    sums = lax.dot_general(
        packed[:, wide:], packed[:, :wide], (((0,), (0,)), ((), ())),
        preferred_element_type=jnp.float32,
    )
    coded, basis = encode(sums, narrow_basis, wide_values, held, workers)
    coded = lax.all_to_all(coded, WK, 0, 0, tiled=True)
    precond = middle(worker, coded, basis, narrow_values, total_tokens)
    precond = lax.all_to_all(precond, WK, 0, 0, tiled=True)
    spread = last(precond, narrow_basis, groups // 2)
    spread = lax.all_to_all(spread, ("x", "yl"), 0, 0, tiled=True)
    other = lax.ppermute(spread, "core", [(0, 1), (1, 0)])
    placed = place(owned_layer, core, spread)
    return place(owned_layer, 1 - core, other, placed)


def solution(mesh):
    fine = Mesh(
        mesh.devices.reshape(4, 2, 2, 8, 2), ("x", "yl", "core", "z", "yh")
    )
    return jax.shard_map(
        local,
        mesh=fine,
        in_specs=(
            P(),
            P(None, GRP + WK, None),
            P(None, GRP + WK, None),
            P(GRP, WK, None),
            P(GRP, None, None),
            P(GRP, WK),
            P(GRP, None),
        ),
        out_specs=P(None, WK, None),
        check_vma=False,
    )
```

```python
import functools

import jax
import jax.numpy as jnp
from jax import lax
from jax.experimental import pallas as pl
from jax.experimental.pallas import tpu as pltpu
from jax.sharding import Mesh, PartitionSpec as P

DAMPING = 0.001
LIMIT = float(2**16 - 1)
POWER_BIAS = 512
VALUE_UNIT = float(2**33)
GRP = ("x", "yl", "core")
WK = ("z", "yh")
HIGH = lax.Precision.HIGH
PLACE_GRANT = 4 * 2**20
PACK_GRANT = 59 * 2**20
MIDDLE_GRANT = 24 * 2**20
ENCODE_GRANT = 47 * 2**20


def pack_kernel(owned_ref, wide_ref, narrow_ref, out_ref, stage_ref, load_sems, store_sems):
    layers, _, wide = wide_ref.shape
    narrow = narrow_ref.shape[2]
    loads, stores = [], []
    for group in range(layers):
        layer = owned_ref[group]
        stage = stage_ref.at[group]
        loads.append(
            (
                pltpu.make_async_copy(
                    wide_ref.at[layer], stage.at[:, pl.ds(0, wide)], load_sems.at[group, 0]
                ),
                pltpu.make_async_copy(
                    narrow_ref.at[layer], stage.at[:, pl.ds(wide, narrow)], load_sems.at[group, 1]
                ),
            )
        )
        stores.append(pltpu.make_async_copy(stage, out_ref.at[group], store_sems.at[group]))
    for pair in loads:
        pair[0].start()
        pair[1].start()
    for pair, store in zip(loads, stores):
        pair[0].wait()
        pair[1].wait()
        store.start()
    for store in stores:
        store.wait()


def pack_tokens(owned_layer, wide_side, narrow_side):
    layers, tokens, wide = wide_side.shape
    narrow = narrow_side.shape[2]
    packed = (layers, tokens, wide + narrow)
    return pl.pallas_call(
        pack_kernel,
        out_shape=jax.ShapeDtypeStruct(packed, wide_side.dtype),
        in_specs=[
            pl.BlockSpec(memory_space=pltpu.SMEM),
            pl.BlockSpec(memory_space=pl.ANY),
            pl.BlockSpec(memory_space=pl.ANY),
        ],
        out_specs=pl.BlockSpec(memory_space=pl.ANY),
        scratch_shapes=[
            pltpu.VMEM(packed, wide_side.dtype),
            pltpu.SemaphoreType.DMA((layers, 2)),
            pltpu.SemaphoreType.DMA((layers,)),
        ],
        compiler_params=pltpu.CompilerParams(vmem_limit_bytes=PACK_GRANT),
    )(owned_layer, wide_side, narrow_side)


def place_kernel(owned_ref, which_ref, blocks_ref, *rest):
    out_ref, sems = rest[-2:]
    which = which_ref[0]
    copies = [
        pltpu.make_async_copy(
            blocks_ref.at[chip], out_ref.at[owned_ref[2 * chip + which]], sems.at[chip]
        )
        for chip in range(blocks_ref.shape[0])
    ]
    for copy in copies:
        copy.start()
    for copy in copies:
        copy.wait()


def place(owned_layer, which, blocks, into=None):
    chips, rows, narrow = blocks.shape
    more = () if into is None else (into,)
    return pl.pallas_call(
        place_kernel,
        out_shape=jax.ShapeDtypeStruct((2 * chips, rows, narrow), blocks.dtype),
        in_specs=[
            pl.BlockSpec(memory_space=pltpu.SMEM),
            pl.BlockSpec(memory_space=pltpu.SMEM),
            pl.BlockSpec(memory_space=pltpu.VMEM),
        ]
        + [pl.BlockSpec(memory_space=pl.ANY)] * len(more),
        out_specs=pl.BlockSpec(memory_space=pl.ANY),
        input_output_aliases={3: 0} if more else {},
        scratch_shapes=[pltpu.SemaphoreType.DMA((chips,))],
        compiler_params=pltpu.CompilerParams(vmem_limit_bytes=PLACE_GRANT),
    )(owned_layer, which, blocks, *more)


def split(value):
    high = value.astype(jnp.bfloat16)
    return high, (value - high.astype(jnp.float32)).astype(jnp.bfloat16)


def product(value, high, low, contract):
    rows = value.shape[0]
    dims = (((1,), (contract,)), ((), ()))
    value_high, value_low = split(value)
    both = lax.dot_general(
        jnp.concatenate([value_high, value_low], axis=0), high, dims,
        preferred_element_type=jnp.float32,
    )
    rest = lax.dot_general(value_high, low, dims, preferred_element_type=jnp.float32)
    return both[:rows] + both[rows:] + rest


def encode_kernel(sums_ref, small_ref, values_ref, held_ref, out_ref, basis_ref, sems):
    loads = [
        pltpu.make_async_copy(held_ref.at[z], basis_ref.at[z], sems.at[z])
        for z in range(held_ref.shape[0])
    ]
    for load in loads:
        load.start()
    workers = out_ref.shape[0]
    narrow = small_ref.shape[1]
    rows = narrow // workers
    half = rows // 2
    tiles = sums_ref.shape[1] // 128
    base = tiles * half
    lane = lax.broadcasted_iota(jnp.int32, (half, 128), 1)
    values = (values_ref[...] * VALUE_UNIT).astype(jnp.int32)
    values = jnp.concatenate([values, jnp.zeros_like(values)], axis=1)
    values = jnp.broadcast_to(values, (half, 128))
    sublane = lax.broadcasted_iota(jnp.int32, (half, 128), 0)
    values = jnp.where(sublane < half // 2, values >> 15, values & 0x7FFF)
    high, low_part = split(sums_ref[...])
    parts = product(small_ref[0].T, high, low_part, 0)
    for worker in range(workers):
        part = parts[worker * rows : (worker + 1) * rows, :]
        most = jnp.max(jnp.abs(part), axis=1, keepdims=True)
        power = jnp.ceil(jnp.log2(jnp.maximum(most, 2.0**-120)))
        code = jnp.floor(part * jnp.exp2(-power) * LIMIT + 0.5).astype(jnp.int32)
        low = jnp.zeros((half, 128), jnp.int32)
        for tile in range(tiles):
            piece = code[:, tile * 128 : (tile + 1) * 128]
            first, second = piece[:half], piece[half:]
            out_ref[worker, tile * half : (tile + 1) * half, :] = ((first >> 1) << 16) | (
                (second >> 1) & 0xFFFF
            )
            low = low | ((first & 1) << (2 * tile)) | ((second & 1) << (2 * tile + 1))
        power = power.astype(jnp.int32) + POWER_BIAS
        more = jnp.where(lane < 64, values, jnp.where(lane < 96, power[:half], power[half:]))
        out_ref[worker, base:, :] = low | (more << 16)
    for load in loads:
        load.wait()


def encode(sums, narrow_basis, wide_values, held, workers):
    narrow, wide = sums.shape
    words = (narrow // workers // 2) * (wide // 128 + 1)
    return pl.pallas_call(
        encode_kernel,
        out_shape=(
            jax.ShapeDtypeStruct((workers, words, 128), jnp.int32),
            jax.ShapeDtypeStruct(held.shape, held.dtype),
        ),
        in_specs=[pl.BlockSpec(memory_space=pltpu.VMEM)] * 3 + [pl.BlockSpec(memory_space=pl.ANY)],
        out_specs=(pl.BlockSpec(memory_space=pltpu.VMEM), pl.BlockSpec(memory_space=pltpu.VMEM)),
        scratch_shapes=[pltpu.SemaphoreType.DMA((held.shape[0],))],
        compiler_params=pltpu.CompilerParams(vmem_limit_bytes=ENCODE_GRANT),
    )(sums, narrow_basis, wide_values, held)


def middle_kernel(total_tokens, worker_ref, coded_ref, basis_ref, small_ref, out_ref):
    workers, words, _ = coded_ref.shape
    half = 8
    tiles = words // half - 1
    base = tiles * half
    lane = lax.broadcasted_iota(jnp.int32, (half, 128), 1)
    sums = [[jnp.zeros((half, 128), jnp.float32) for _ in range(tiles)] for _ in range(2)]
    values = []
    for worker in range(workers):
        low = coded_ref[worker, base:, :]
        tail = ((low >> 16) & 0xFFFF).astype(jnp.float32)
        value = tail[:1] * 2.0**15 + tail[half // 2 : half // 2 + 1]
        values.append(jnp.broadcast_to(value * (1.0 / VALUE_UNIT), (half, 128)))
        units = [jnp.exp2(tail[:, at : at + 1] - POWER_BIAS) for at in (64, 96)]
        for tile in range(tiles):
            word = coded_ref[worker, tile * half : (tile + 1) * half, :]
            first = ((word >> 16) << 1) | ((low >> (2 * tile)) & 1)
            second = (((word << 16) >> 16) << 1) | ((low >> (2 * tile + 1)) & 1)
            sums[0][tile] += first.astype(jnp.float32) * units[0]
            sums[1][tile] += second.astype(jnp.float32) * units[1]
    gradient = jnp.concatenate(
        [jnp.concatenate(part, axis=1) for part in sums], axis=0
    ) * (1.0 / (LIMIT * total_tokens))
    wide_values = jnp.concatenate(
        [
            jnp.where(lane < 64, values[2 * tile], pltpu.roll(values[2 * tile + 1], 64, 1))
            for tile in range(tiles)
        ],
        axis=1,
    )[:1]
    count = small_ref.shape[1]
    own = lax.broadcasted_iota(jnp.int32, (2 * half, count), 1) == (
        worker_ref[0] * (2 * half) + lax.broadcasted_iota(jnp.int32, (2 * half, count), 0)
    )
    small = jnp.sum(jnp.where(own, small_ref[...], 0.0), axis=1, keepdims=True)
    high, low = (
        jnp.concatenate(
            [basis_ref[z, h, i] for z in range(basis_ref.shape[0]) for h in range(basis_ref.shape[1])],
            axis=0,
        )
        for i in range(2)
    )
    rotated = product(gradient, high, low, 0)
    scaled = rotated / (small * wide_values + DAMPING)
    precond = product(scaled, high, low, 1)
    for tile in range(tiles):
        piece = precond[:, tile * 128 : (tile + 1) * 128]
        first, second = piece[:half], piece[half:]
        out_ref[2 * tile] = jnp.where(lane < 64, first, pltpu.roll(second, 64, 1))
        out_ref[2 * tile + 1] = jnp.where(lane < 64, pltpu.roll(first, 64, 1), second)


def middle(worker, coded, basis, narrow_values, total_tokens):
    return pl.pallas_call(
        functools.partial(middle_kernel, total_tokens),
        out_shape=jax.ShapeDtypeStruct((coded.shape[0], 8, 128), jnp.float32),
        in_specs=[pl.BlockSpec(memory_space=pltpu.SMEM)] + [pl.BlockSpec(memory_space=pltpu.VMEM)] * 3,
        out_specs=pl.BlockSpec(memory_space=pltpu.VMEM),
        compiler_params=pltpu.CompilerParams(vmem_limit_bytes=MIDDLE_GRANT),
    )(worker, coded, basis, narrow_values)


def last_kernel(precond_ref, small_ref, out_ref):
    pieces = []
    for worker in range(precond_ref.shape[0]):
        block = precond_ref[worker]
        pieces += [block[:, :64], block[:, 64:]]
    columns = jnp.concatenate(pieces, axis=0)
    mine = lax.dot_general(
        columns.T, small_ref[0], (((1,), (1,)), ((), ())),
        precision=lax.Precision.HIGHEST, preferred_element_type=jnp.float32,
    )
    for chip in range(out_ref.shape[0]):
        out_ref[chip] = mine


def last(precond, narrow_basis, chips):
    return pl.pallas_call(
        last_kernel,
        out_shape=jax.ShapeDtypeStruct((chips, 64, narrow_basis.shape[1]), jnp.float32),
        in_specs=[pl.BlockSpec(memory_space=pltpu.VMEM)] * 2,
        out_specs=pl.BlockSpec(memory_space=pltpu.VMEM),
        compiler_params=pltpu.CompilerParams(vmem_limit_bytes=4 * 2**20),
    )(precond, narrow_basis)


def local(
    owned_layer, wide_side, narrow_side, wide_basis, narrow_basis, wide_values, narrow_values
):
    groups = lax.axis_size(GRP)
    workers = lax.axis_size(WK)
    layers, tokens, wide = wide_side.shape
    narrow = narrow_side.shape[2]
    total_tokens = tokens * groups * workers

    swapped = lax.ppermute(wide_basis[0], "yh", [(0, 1), (1, 0)])
    packed = pack_tokens(owned_layer, wide_side, narrow_side)
    low = lax.axis_index("yh") == 0
    held = jnp.stack(
        [jnp.where(low, wide_basis[0], swapped), jnp.where(low, swapped, wide_basis[0])]
    )
    high = lax.reduce_precision(held, 8, 7)
    held = jnp.stack([high.astype(jnp.bfloat16), (held - high).astype(jnp.bfloat16)], axis=1)
    worker = lax.axis_index(WK).reshape(1)
    core = lax.axis_index("core").reshape(1)
    held, packed, worker, core = lax.optimization_barrier((held, packed, worker, core))
    held = lax.all_gather(held, "z", axis=0, tiled=False)

    packed = lax.all_to_all(packed, GRP, 0, 0, tiled=True)
    packed = packed.reshape(groups * tokens, wide + narrow)
    sums = lax.dot_general(
        packed[:, wide:], packed[:, :wide], (((0,), (0,)), ((), ())),
        preferred_element_type=jnp.float32,
    )
    coded, basis = encode(sums, narrow_basis, wide_values, held, workers)
    coded = lax.all_to_all(coded, WK, 0, 0, tiled=True)
    precond = middle(worker, coded, basis, narrow_values, total_tokens)
    precond = lax.all_to_all(precond, WK, 0, 0, tiled=True)
    spread = last(precond, narrow_basis, groups // 2)
    spread = lax.all_to_all(spread, ("x", "yl"), 0, 0, tiled=True)
    other = lax.ppermute(spread, "core", [(0, 1), (1, 0)])
    placed = place(owned_layer, core, spread)
    return place(owned_layer, 1 - core, other, placed)


def solution(mesh):
    fine = Mesh(
        mesh.devices.reshape(4, 2, 2, 8, 2), ("x", "yl", "core", "z", "yh")
    )
    return jax.shard_map(
        local,
        mesh=fine,
        in_specs=(
            P(),
            P(None, GRP + WK, None),
            P(None, GRP + WK, None),
            P(GRP, WK, None),
            P(GRP, None, None),
            P(GRP, WK),
            P(GRP, None),
        ),
        out_specs=P(None, WK, None),
        check_vma=False,
    )
```

```python
import functools

import jax
import jax.numpy as jnp
from jax import lax
from jax.experimental import pallas as pl
from jax.experimental.pallas import tpu as pltpu
from jax.sharding import Mesh, PartitionSpec as P

DAMPING = 0.001
LIMIT = float(2**16 - 1)
POWER_BIAS = 512
VALUE_UNIT = float(2**33)
GRP = ("x", "yl", "core")
WK = ("z", "yh")
HIGH = lax.Precision.HIGH
PLACE_GRANT = 4 * 2**20
PACK_GRANT = 59 * 2**20
MIDDLE_GRANT = 24 * 2**20
ENCODE_GRANT = 47 * 2**20


def pack_kernel(owned_ref, wide_ref, narrow_ref, out_ref, stage_ref, load_sems, store_sems):
    layers, _, wide = wide_ref.shape
    narrow = narrow_ref.shape[2]
    loads, stores = [], []
    for group in range(layers):
        layer = owned_ref[group]
        stage = stage_ref.at[group]
        loads.append(
            (
                pltpu.make_async_copy(
                    wide_ref.at[layer], stage.at[:, pl.ds(0, wide)], load_sems.at[group, 0]
                ),
                pltpu.make_async_copy(
                    narrow_ref.at[layer], stage.at[:, pl.ds(wide, narrow)], load_sems.at[group, 1]
                ),
            )
        )
        stores.append(pltpu.make_async_copy(stage, out_ref.at[group], store_sems.at[group]))
    for pair in loads:
        pair[0].start()
        pair[1].start()
    for pair, store in zip(loads, stores):
        pair[0].wait()
        pair[1].wait()
        store.start()
    for store in stores:
        store.wait()


def pack_tokens(owned_layer, wide_side, narrow_side):
    layers, tokens, wide = wide_side.shape
    narrow = narrow_side.shape[2]
    packed = (layers, tokens, wide + narrow)
    return pl.pallas_call(
        pack_kernel,
        out_shape=jax.ShapeDtypeStruct(packed, wide_side.dtype),
        in_specs=[
            pl.BlockSpec(memory_space=pltpu.SMEM),
            pl.BlockSpec(memory_space=pl.ANY),
            pl.BlockSpec(memory_space=pl.ANY),
        ],
        out_specs=pl.BlockSpec(memory_space=pl.ANY),
        scratch_shapes=[
            pltpu.VMEM(packed, wide_side.dtype),
            pltpu.SemaphoreType.DMA((layers, 2)),
            pltpu.SemaphoreType.DMA((layers,)),
        ],
        compiler_params=pltpu.CompilerParams(vmem_limit_bytes=PACK_GRANT),
    )(owned_layer, wide_side, narrow_side)


def place_kernel(owned_ref, which_ref, blocks_ref, *rest):
    out_ref, sems = rest[-2:]
    which = which_ref[0]
    copies = [
        pltpu.make_async_copy(
            blocks_ref.at[chip], out_ref.at[owned_ref[2 * chip + which]], sems.at[chip]
        )
        for chip in range(blocks_ref.shape[0])
    ]
    for copy in copies:
        copy.start()
    for copy in copies:
        copy.wait()


def place(owned_layer, which, blocks, into=None):
    chips, rows, narrow = blocks.shape
    more = () if into is None else (into,)
    return pl.pallas_call(
        place_kernel,
        out_shape=jax.ShapeDtypeStruct((2 * chips, rows, narrow), blocks.dtype),
        in_specs=[
            pl.BlockSpec(memory_space=pltpu.SMEM),
            pl.BlockSpec(memory_space=pltpu.SMEM),
            pl.BlockSpec(memory_space=pltpu.VMEM),
        ]
        + [pl.BlockSpec(memory_space=pl.ANY)] * len(more),
        out_specs=pl.BlockSpec(memory_space=pl.ANY),
        input_output_aliases={3: 0} if more else {},
        scratch_shapes=[pltpu.SemaphoreType.DMA((chips,))],
        compiler_params=pltpu.CompilerParams(vmem_limit_bytes=PLACE_GRANT),
    )(owned_layer, which, blocks, *more)


def split(value):
    high = value.astype(jnp.bfloat16)
    return high, (value - high.astype(jnp.float32)).astype(jnp.bfloat16)


def product(value, high, low, contract):
    rows = value.shape[0]
    dims = (((1,), (contract,)), ((), ()))
    value_high, value_low = split(value)
    both = lax.dot_general(
        jnp.concatenate([value_high, value_low], axis=0), high, dims,
        preferred_element_type=jnp.float32,
    )
    rest = lax.dot_general(value_high, low, dims, preferred_element_type=jnp.float32)
    return both[:rows] + both[rows:] + rest


def encode_kernel(sums_ref, small_ref, values_ref, held_ref, out_ref, basis_ref, sems):
    loads = [
        pltpu.make_async_copy(held_ref.at[z], basis_ref.at[z], sems.at[z])
        for z in range(held_ref.shape[0])
    ]
    for load in loads:
        load.start()
    workers = out_ref.shape[0]
    narrow = small_ref.shape[1]
    rows = narrow // workers
    half = rows // 2
    tiles = sums_ref.shape[1] // 128
    base = tiles * half
    lane = lax.broadcasted_iota(jnp.int32, (half, 128), 1)
    values = (values_ref[...] * VALUE_UNIT).astype(jnp.int32)
    values = jnp.concatenate([values, jnp.zeros_like(values)], axis=1)
    values = jnp.broadcast_to(values, (half, 128))
    sublane = lax.broadcasted_iota(jnp.int32, (half, 128), 0)
    values = jnp.where(sublane < half // 2, values >> 15, values & 0x7FFF)
    high, low_part = split(sums_ref[...])
    parts = product(small_ref[0].T, high, low_part, 0)
    for worker in range(workers):
        part = parts[worker * rows : (worker + 1) * rows, :]
        most = jnp.max(jnp.abs(part), axis=1, keepdims=True)
        power = jnp.ceil(jnp.log2(jnp.maximum(most, 2.0**-120)))
        code = jnp.floor(part * jnp.exp2(-power) * LIMIT + 0.5).astype(jnp.int32)
        low = jnp.zeros((half, 128), jnp.int32)
        for tile in range(tiles):
            piece = code[:, tile * 128 : (tile + 1) * 128]
            first, second = piece[:half], piece[half:]
            out_ref[worker, tile * half : (tile + 1) * half, :] = ((first >> 1) << 16) | (
                (second >> 1) & 0xFFFF
            )
            low = low | ((first & 1) << (2 * tile)) | ((second & 1) << (2 * tile + 1))
        power = power.astype(jnp.int32) + POWER_BIAS
        more = jnp.where(lane < 64, values, jnp.where(lane < 96, power[:half], power[half:]))
        out_ref[worker, base:, :] = low | (more << 16)
    for load in loads:
        load.wait()


def encode(sums, narrow_basis, wide_values, held, workers):
    narrow, wide = sums.shape
    words = (narrow // workers // 2) * (wide // 128 + 1)
    return pl.pallas_call(
        encode_kernel,
        out_shape=(
            jax.ShapeDtypeStruct((workers, words, 128), jnp.int32),
            jax.ShapeDtypeStruct(held.shape, held.dtype),
        ),
        in_specs=[pl.BlockSpec(memory_space=pltpu.VMEM)] * 3 + [pl.BlockSpec(memory_space=pl.ANY)],
        out_specs=(pl.BlockSpec(memory_space=pltpu.VMEM), pl.BlockSpec(memory_space=pltpu.VMEM)),
        scratch_shapes=[pltpu.SemaphoreType.DMA((held.shape[0],))],
        compiler_params=pltpu.CompilerParams(vmem_limit_bytes=ENCODE_GRANT),
    )(sums, narrow_basis, wide_values, held)


def middle_kernel(total_tokens, worker_ref, coded_ref, basis_ref, small_ref, out_ref):
    workers, words, _ = coded_ref.shape
    half = 8
    tiles = words // half - 1
    base = tiles * half
    lane = lax.broadcasted_iota(jnp.int32, (half, 128), 1)
    sums = [[jnp.zeros((half, 128), jnp.float32) for _ in range(tiles)] for _ in range(2)]
    values = []
    for worker in range(workers):
        low = coded_ref[worker, base:, :]
        tail = ((low >> 16) & 0xFFFF).astype(jnp.float32)
        value = tail[:1] * 2.0**15 + tail[half // 2 : half // 2 + 1]
        values.append(jnp.broadcast_to(value * (1.0 / VALUE_UNIT), (half, 128)))
        units = [jnp.exp2(tail[:, at : at + 1] - POWER_BIAS) for at in (64, 96)]
        for tile in range(tiles):
            word = coded_ref[worker, tile * half : (tile + 1) * half, :]
            first = ((word >> 16) << 1) | ((low >> (2 * tile)) & 1)
            second = (((word << 16) >> 16) << 1) | ((low >> (2 * tile + 1)) & 1)
            sums[0][tile] += first.astype(jnp.float32) * units[0]
            sums[1][tile] += second.astype(jnp.float32) * units[1]
    gradient = jnp.concatenate(
        [jnp.concatenate(part, axis=1) for part in sums], axis=0
    ) * (1.0 / (LIMIT * total_tokens))
    wide_values = jnp.concatenate(
        [
            jnp.where(lane < 64, values[2 * tile], pltpu.roll(values[2 * tile + 1], 64, 1))
            for tile in range(tiles)
        ],
        axis=1,
    )[:1]
    count = small_ref.shape[1]
    own = lax.broadcasted_iota(jnp.int32, (2 * half, count), 1) == (
        worker_ref[0] * (2 * half) + lax.broadcasted_iota(jnp.int32, (2 * half, count), 0)
    )
    small = jnp.sum(jnp.where(own, small_ref[...], 0.0), axis=1, keepdims=True)
    high, low = (
        jnp.concatenate(
            [basis_ref[z, h, i] for z in range(basis_ref.shape[0]) for h in range(basis_ref.shape[1])],
            axis=0,
        )
        for i in range(2)
    )
    rotated = product(gradient, high, low, 0)
    scaled = rotated / (small * wide_values + DAMPING)
    precond = product(scaled, high, low, 1)
    for tile in range(tiles):
        piece = precond[:, tile * 128 : (tile + 1) * 128]
        first, second = piece[:half], piece[half:]
        out_ref[2 * tile] = jnp.where(lane < 64, first, pltpu.roll(second, 64, 1))
        out_ref[2 * tile + 1] = jnp.where(lane < 64, pltpu.roll(first, 64, 1), second)


def middle(worker, coded, basis, narrow_values, total_tokens):
    return pl.pallas_call(
        functools.partial(middle_kernel, total_tokens),
        out_shape=jax.ShapeDtypeStruct((coded.shape[0], 8, 128), jnp.float32),
        in_specs=[pl.BlockSpec(memory_space=pltpu.SMEM)] + [pl.BlockSpec(memory_space=pltpu.VMEM)] * 3,
        out_specs=pl.BlockSpec(memory_space=pltpu.VMEM),
        compiler_params=pltpu.CompilerParams(vmem_limit_bytes=MIDDLE_GRANT),
    )(worker, coded, basis, narrow_values)


def last_kernel(precond_ref, small_ref, out_ref):
    pieces = []
    for worker in range(precond_ref.shape[0]):
        block = precond_ref[worker]
        pieces += [block[:, :64], block[:, 64:]]
    columns = jnp.concatenate(pieces, axis=0)
    mine = lax.dot_general(
        columns.T, small_ref[0], (((1,), (1,)), ((), ())),
        precision=lax.Precision.HIGHEST, preferred_element_type=jnp.float32,
    )
    for chip in range(out_ref.shape[0]):
        out_ref[chip] = mine


def last(precond, narrow_basis, chips):
    return pl.pallas_call(
        last_kernel,
        out_shape=jax.ShapeDtypeStruct((chips, 64, narrow_basis.shape[1]), jnp.float32),
        in_specs=[pl.BlockSpec(memory_space=pltpu.VMEM)] * 2,
        out_specs=pl.BlockSpec(memory_space=pltpu.VMEM),
        compiler_params=pltpu.CompilerParams(vmem_limit_bytes=4 * 2**20),
    )(precond, narrow_basis)


def two_parts(value):
    high = lax.reduce_precision(value, 8, 7)
    return jnp.stack([high.astype(jnp.bfloat16), (value - high).astype(jnp.bfloat16)])


def local(
    owned_layer, wide_side, narrow_side, wide_basis, narrow_basis, wide_values, narrow_values
):
    groups = lax.axis_size(GRP)
    workers = lax.axis_size(WK)
    layers, tokens, wide = wide_side.shape
    narrow = narrow_side.shape[2]
    total_tokens = tokens * groups * workers

    swapped = lax.ppermute(wide_basis[0], "yh", [(0, 1), (1, 0)])
    packed = pack_tokens(owned_layer, wide_side, narrow_side)
    half = lax.axis_index("yh")
    own = two_parts(wide_basis[0])
    held = jnp.zeros((2,) + own.shape, own.dtype)
    held = lax.dynamic_update_slice(held, own[None], (half, 0, 0, 0))
    held = lax.optimization_barrier(held)
    held = lax.dynamic_update_slice(held, two_parts(swapped)[None], (1 - half, 0, 0, 0))
    worker = lax.axis_index(WK).reshape(1)
    core = lax.axis_index("core").reshape(1)
    held, packed, worker, core = lax.optimization_barrier((held, packed, worker, core))
    held = lax.all_gather(held, "z", axis=0, tiled=False)

    packed = lax.all_to_all(packed, GRP, 0, 0, tiled=True)
    packed = packed.reshape(groups * tokens, wide + narrow)
    sums = lax.dot_general(
        packed[:, wide:], packed[:, :wide], (((0,), (0,)), ((), ())),
        preferred_element_type=jnp.float32,
    )
    coded, basis = encode(sums, narrow_basis, wide_values, held, workers)
    coded = lax.all_to_all(coded, WK, 0, 0, tiled=True)
    precond = middle(worker, coded, basis, narrow_values, total_tokens)
    precond = lax.all_to_all(precond, WK, 0, 0, tiled=True)
    spread = last(precond, narrow_basis, groups // 2)
    spread = lax.all_to_all(spread, ("x", "yl"), 0, 0, tiled=True)
    other = lax.ppermute(spread, "core", [(0, 1), (1, 0)])
    placed = place(owned_layer, core, spread)
    return place(owned_layer, 1 - core, other, placed)


def solution(mesh):
    fine = Mesh(
        mesh.devices.reshape(4, 2, 2, 8, 2), ("x", "yl", "core", "z", "yh")
    )
    return jax.shard_map(
        local,
        mesh=fine,
        in_specs=(
            P(),
            P(None, GRP + WK, None),
            P(None, GRP + WK, None),
            P(GRP, WK, None),
            P(GRP, None, None),
            P(GRP, WK),
            P(GRP, None),
        ),
        out_specs=P(None, WK, None),
        check_vma=False,
    )
```

```python
import functools

import jax
import jax.numpy as jnp
from jax import lax
from jax.experimental import pallas as pl
from jax.experimental.pallas import tpu as pltpu
from jax.sharding import Mesh, PartitionSpec as P

DAMPING = 0.001
LIMIT = float(2**16 - 1)
POWER_BIAS = 512
VALUE_UNIT = float(2**33)
GRP = ("x", "yl", "core")
WK = ("z", "yh")
HIGH = lax.Precision.HIGH
PLACE_GRANT = 4 * 2**20
PACK_GRANT = 59 * 2**20
MIDDLE_GRANT = 24 * 2**20
ENCODE_GRANT = 47 * 2**20


def pack_kernel(owned_ref, wide_ref, narrow_ref, out_ref, stage_ref, load_sems, store_sems):
    layers, _, wide = wide_ref.shape
    narrow = narrow_ref.shape[2]
    loads, stores = [], []
    for group in range(layers):
        layer = owned_ref[group]
        stage = stage_ref.at[group]
        loads.append(
            (
                pltpu.make_async_copy(
                    wide_ref.at[layer], stage.at[:, pl.ds(0, wide)], load_sems.at[group, 0]
                ),
                pltpu.make_async_copy(
                    narrow_ref.at[layer], stage.at[:, pl.ds(wide, narrow)], load_sems.at[group, 1]
                ),
            )
        )
        stores.append(pltpu.make_async_copy(stage, out_ref.at[group], store_sems.at[group]))
    for pair in loads:
        pair[0].start()
        pair[1].start()
    for pair, store in zip(loads, stores):
        pair[0].wait()
        pair[1].wait()
        store.start()
    for store in stores:
        store.wait()


def pack_tokens(owned_layer, wide_side, narrow_side):
    layers, tokens, wide = wide_side.shape
    narrow = narrow_side.shape[2]
    packed = (layers, tokens, wide + narrow)
    return pl.pallas_call(
        pack_kernel,
        out_shape=jax.ShapeDtypeStruct(packed, wide_side.dtype),
        in_specs=[
            pl.BlockSpec(memory_space=pltpu.SMEM),
            pl.BlockSpec(memory_space=pl.ANY),
            pl.BlockSpec(memory_space=pl.ANY),
        ],
        out_specs=pl.BlockSpec(memory_space=pl.ANY),
        scratch_shapes=[
            pltpu.VMEM(packed, wide_side.dtype),
            pltpu.SemaphoreType.DMA((layers, 2)),
            pltpu.SemaphoreType.DMA((layers,)),
        ],
        compiler_params=pltpu.CompilerParams(vmem_limit_bytes=PACK_GRANT),
    )(owned_layer, wide_side, narrow_side)


def place_kernel(owned_ref, which_ref, blocks_ref, *rest):
    out_ref, sems = rest[-2:]
    which = which_ref[0]
    copies = [
        pltpu.make_async_copy(
            blocks_ref.at[chip], out_ref.at[owned_ref[2 * chip + which]], sems.at[chip]
        )
        for chip in range(blocks_ref.shape[0])
    ]
    for copy in copies:
        copy.start()
    for copy in copies:
        copy.wait()


def place(owned_layer, which, blocks, into=None):
    chips, rows, narrow = blocks.shape
    more = () if into is None else (into,)
    return pl.pallas_call(
        place_kernel,
        out_shape=jax.ShapeDtypeStruct((2 * chips, rows, narrow), blocks.dtype),
        in_specs=[
            pl.BlockSpec(memory_space=pltpu.SMEM),
            pl.BlockSpec(memory_space=pltpu.SMEM),
            pl.BlockSpec(memory_space=pltpu.VMEM),
        ]
        + [pl.BlockSpec(memory_space=pl.ANY)] * len(more),
        out_specs=pl.BlockSpec(memory_space=pl.ANY),
        input_output_aliases={3: 0} if more else {},
        scratch_shapes=[pltpu.SemaphoreType.DMA((chips,))],
        compiler_params=pltpu.CompilerParams(vmem_limit_bytes=PLACE_GRANT),
    )(owned_layer, which, blocks, *more)


def split(value):
    high = value.astype(jnp.bfloat16)
    return high, (value - high.astype(jnp.float32)).astype(jnp.bfloat16)


def product(value, high, low, contract):
    rows = value.shape[0]
    dims = (((1,), (contract,)), ((), ()))
    value_high, value_low = split(value)
    both = lax.dot_general(
        jnp.concatenate([value_high, value_low], axis=0), high, dims,
        preferred_element_type=jnp.float32,
    )
    rest = lax.dot_general(value_high, low, dims, preferred_element_type=jnp.float32)
    return both[:rows] + both[rows:] + rest


def encode_kernel(sums_ref, small_ref, values_ref, held_ref, out_ref, basis_ref, sems):
    loads = [
        pltpu.make_async_copy(
            held_ref.at[z, h, i], basis_ref.at[i, pl.ds((2 * z + h) * 64, 64)], sems.at[i, 2 * z + h]
        )
        for i in range(2)
        for z in range(held_ref.shape[0])
        for h in range(2)
    ]
    for load in loads:
        load.start()
    workers = out_ref.shape[0]
    narrow = small_ref.shape[1]
    rows = narrow // workers
    half = rows // 2
    tiles = sums_ref.shape[1] // 128
    base = tiles * half
    lane = lax.broadcasted_iota(jnp.int32, (half, 128), 1)
    values = (values_ref[...] * VALUE_UNIT).astype(jnp.int32)
    values = jnp.concatenate([values, jnp.zeros_like(values)], axis=1)
    values = jnp.broadcast_to(values, (half, 128))
    sublane = lax.broadcasted_iota(jnp.int32, (half, 128), 0)
    values = jnp.where(sublane < half // 2, values >> 15, values & 0x7FFF)
    high, low_part = split(sums_ref[...])
    parts = product(small_ref[0].T, high, low_part, 0)
    for worker in range(workers):
        part = parts[worker * rows : (worker + 1) * rows, :]
        most = jnp.max(jnp.abs(part), axis=1, keepdims=True)
        power = jnp.ceil(jnp.log2(jnp.maximum(most, 2.0**-120)))
        code = jnp.floor(part * jnp.exp2(-power) * LIMIT + 0.5).astype(jnp.int32)
        low = jnp.zeros((half, 128), jnp.int32)
        for tile in range(tiles):
            piece = code[:, tile * 128 : (tile + 1) * 128]
            first, second = piece[:half], piece[half:]
            out_ref[worker, tile * half : (tile + 1) * half, :] = ((first >> 1) << 16) | (
                (second >> 1) & 0xFFFF
            )
            low = low | ((first & 1) << (2 * tile)) | ((second & 1) << (2 * tile + 1))
        power = power.astype(jnp.int32) + POWER_BIAS
        more = jnp.where(lane < 64, values, jnp.where(lane < 96, power[:half], power[half:]))
        out_ref[worker, base:, :] = low | (more << 16)
    for load in loads:
        load.wait()


def encode(sums, narrow_basis, wide_values, held, workers):
    narrow, wide = sums.shape
    words = (narrow // workers // 2) * (wide // 128 + 1)
    return pl.pallas_call(
        encode_kernel,
        out_shape=(
            jax.ShapeDtypeStruct((workers, words, 128), jnp.int32),
            jax.ShapeDtypeStruct((2, wide, wide), held.dtype),
        ),
        in_specs=[pl.BlockSpec(memory_space=pltpu.VMEM)] * 3 + [pl.BlockSpec(memory_space=pl.ANY)],
        out_specs=(pl.BlockSpec(memory_space=pltpu.VMEM), pl.BlockSpec(memory_space=pltpu.VMEM)),
        scratch_shapes=[pltpu.SemaphoreType.DMA((2, workers))],
        compiler_params=pltpu.CompilerParams(vmem_limit_bytes=ENCODE_GRANT),
    )(sums, narrow_basis, wide_values, held)


def middle_kernel(total_tokens, worker_ref, coded_ref, basis_ref, small_ref, out_ref):
    workers, words, _ = coded_ref.shape
    half = 8
    tiles = words // half - 1
    base = tiles * half
    lane = lax.broadcasted_iota(jnp.int32, (half, 128), 1)
    sums = [[jnp.zeros((half, 128), jnp.float32) for _ in range(tiles)] for _ in range(2)]
    values = []
    for worker in range(workers):
        low = coded_ref[worker, base:, :]
        tail = ((low >> 16) & 0xFFFF).astype(jnp.float32)
        value = tail[:1] * 2.0**15 + tail[half // 2 : half // 2 + 1]
        values.append(jnp.broadcast_to(value * (1.0 / VALUE_UNIT), (half, 128)))
        units = [jnp.exp2(tail[:, at : at + 1] - POWER_BIAS) for at in (64, 96)]
        for tile in range(tiles):
            word = coded_ref[worker, tile * half : (tile + 1) * half, :]
            first = ((word >> 16) << 1) | ((low >> (2 * tile)) & 1)
            second = (((word << 16) >> 16) << 1) | ((low >> (2 * tile + 1)) & 1)
            sums[0][tile] += first.astype(jnp.float32) * units[0]
            sums[1][tile] += second.astype(jnp.float32) * units[1]
    gradient = jnp.concatenate(
        [jnp.concatenate(part, axis=1) for part in sums], axis=0
    ) * (1.0 / (LIMIT * total_tokens))
    wide_values = jnp.concatenate(
        [
            jnp.where(lane < 64, values[2 * tile], pltpu.roll(values[2 * tile + 1], 64, 1))
            for tile in range(tiles)
        ],
        axis=1,
    )[:1]
    count = small_ref.shape[1]
    own = lax.broadcasted_iota(jnp.int32, (2 * half, count), 1) == (
        worker_ref[0] * (2 * half) + lax.broadcasted_iota(jnp.int32, (2 * half, count), 0)
    )
    small = jnp.sum(jnp.where(own, small_ref[...], 0.0), axis=1, keepdims=True)
    high, low = basis_ref[0], basis_ref[1]
    rotated = product(gradient, high, low, 0)
    scaled = rotated / (small * wide_values + DAMPING)
    precond = product(scaled, high, low, 1)
    for tile in range(tiles):
        piece = precond[:, tile * 128 : (tile + 1) * 128]
        first, second = piece[:half], piece[half:]
        out_ref[2 * tile] = jnp.where(lane < 64, first, pltpu.roll(second, 64, 1))
        out_ref[2 * tile + 1] = jnp.where(lane < 64, pltpu.roll(first, 64, 1), second)


def middle(worker, coded, basis, narrow_values, total_tokens):
    return pl.pallas_call(
        functools.partial(middle_kernel, total_tokens),
        out_shape=jax.ShapeDtypeStruct((coded.shape[0], 8, 128), jnp.float32),
        in_specs=[pl.BlockSpec(memory_space=pltpu.SMEM)] + [pl.BlockSpec(memory_space=pltpu.VMEM)] * 3,
        out_specs=pl.BlockSpec(memory_space=pltpu.VMEM),
        compiler_params=pltpu.CompilerParams(vmem_limit_bytes=MIDDLE_GRANT),
    )(worker, coded, basis, narrow_values)


def last_kernel(precond_ref, small_ref, out_ref):
    pieces = []
    for worker in range(precond_ref.shape[0]):
        block = precond_ref[worker]
        pieces += [block[:, :64], block[:, 64:]]
    columns = jnp.concatenate(pieces, axis=0)
    mine = lax.dot_general(
        columns.T, small_ref[0], (((1,), (1,)), ((), ())),
        precision=lax.Precision.HIGHEST, preferred_element_type=jnp.float32,
    )
    for chip in range(out_ref.shape[0]):
        out_ref[chip] = mine


def last(precond, narrow_basis, chips):
    return pl.pallas_call(
        last_kernel,
        out_shape=jax.ShapeDtypeStruct((chips, 64, narrow_basis.shape[1]), jnp.float32),
        in_specs=[pl.BlockSpec(memory_space=pltpu.VMEM)] * 2,
        out_specs=pl.BlockSpec(memory_space=pltpu.VMEM),
        compiler_params=pltpu.CompilerParams(vmem_limit_bytes=4 * 2**20),
    )(precond, narrow_basis)


def local(
    owned_layer, wide_side, narrow_side, wide_basis, narrow_basis, wide_values, narrow_values
):
    groups = lax.axis_size(GRP)
    workers = lax.axis_size(WK)
    layers, tokens, wide = wide_side.shape
    narrow = narrow_side.shape[2]
    total_tokens = tokens * groups * workers

    swapped = lax.ppermute(wide_basis[0], "yh", [(0, 1), (1, 0)])
    packed = pack_tokens(owned_layer, wide_side, narrow_side)
    low = lax.axis_index("yh") == 0
    held = jnp.stack(
        [jnp.where(low, wide_basis[0], swapped), jnp.where(low, swapped, wide_basis[0])]
    )
    high = lax.reduce_precision(held, 8, 7)
    held = jnp.stack([high.astype(jnp.bfloat16), (held - high).astype(jnp.bfloat16)], axis=1)
    worker = lax.axis_index(WK).reshape(1)
    core = lax.axis_index("core").reshape(1)
    held, packed, worker, core = lax.optimization_barrier((held, packed, worker, core))
    held = lax.all_gather(held, "z", axis=0, tiled=False)

    packed = lax.all_to_all(packed, GRP, 0, 0, tiled=True)
    packed = packed.reshape(groups * tokens, wide + narrow)
    sums = lax.dot_general(
        packed[:, wide:], packed[:, :wide], (((0,), (0,)), ((), ())),
        preferred_element_type=jnp.float32,
    )
    coded, basis = encode(sums, narrow_basis, wide_values, held, workers)
    coded = lax.all_to_all(coded, WK, 0, 0, tiled=True)
    precond = middle(worker, coded, basis, narrow_values, total_tokens)
    precond = lax.all_to_all(precond, WK, 0, 0, tiled=True)
    spread = last(precond, narrow_basis, groups // 2)
    spread = lax.all_to_all(spread, ("x", "yl"), 0, 0, tiled=True)
    other = lax.ppermute(spread, "core", [(0, 1), (1, 0)])
    placed = place(owned_layer, core, spread)
    return place(owned_layer, 1 - core, other, placed)


def solution(mesh):
    fine = Mesh(
        mesh.devices.reshape(4, 2, 2, 8, 2), ("x", "yl", "core", "z", "yh")
    )
    return jax.shard_map(
        local,
        mesh=fine,
        in_specs=(
            P(),
            P(None, GRP + WK, None),
            P(None, GRP + WK, None),
            P(GRP, WK, None),
            P(GRP, None, None),
            P(GRP, WK),
            P(GRP, None),
        ),
        out_specs=P(None, WK, None),
        check_vma=False,
    )
```
